32 devices in a mesh: vb: 8 (over z, x), vc: 4 (over y, core).
Axes of the slice: x: 2, y: 2, z: 4, core: 2. Of those that a mesh axis runs over, the one named last changes fastest.
Arguments:
- integrals: float32 [2, 512, 512, 512], P(None, 'vb', 'vc'), may hold values from -0.25 to 0.25
- doubles: float32 [3, 512, 512], P(None, 'vb'), may hold values from -6 to 6
- eps_occ: float32 [100], replicated, may hold values from -2 to -0.5
- eps_virt: float32 [512], replicated, may hold values from 0.2 to 3
- triple: int32 [3], replicated, may hold values from 0 to 99
- energy_order: int32 [512], replicated, may hold values from 0 to 511, each once
Outputs:
- amplitudes: float32 [512, 512, 512], P('vb', 'vc')
- grad: float32 [512, 512], P('vb', 'vc')
The draws below stay inside these ranges and needn't reach their ends.
Inputs may be any that keep to these rules, and one draw needn't show every extreme that they name: `energy_order`: each of 0 to 511 appears once.
All inputs are finite; a program needn't handle non-finite values.
Results may differ from the reference program's by a relative error of at most 0.00007.
Values sent between devices are 32-bit elements; how exact they have to be, the bound alone decides.
No kernel may reach another device: no remote copies, remote signals or barrier semaphores. Data moves between devices by JAX's collectives and lax.ppermute only.
A program may use at most 192 MiB of HBM per device.

```python
import jax
import jax.numpy as jnp
from jax import lax

V = 512
NOCC = 100


def shard_levels(own_key, extent, pieces, smallest, high):
    factor_of = 1.0
    for dim, shards_of in pieces:
        heights = jax.random.uniform(jax.random.fold_in(jax.random.fold_in(own_key, 6), dim), (shards_of,), jnp.float32, smallest / len(pieces), high / len(pieces))
        factor_of = factor_of * jnp.repeat(jnp.exp(heights), extent[dim] // shards_of).reshape((-1,) + (1,) * (len(extent) - 1 - dim))
    return factor_of


def normal_values(own_key, extent, scale, limit, cuts=(), kind=jnp.bfloat16):
    values = scale * jax.random.normal(own_key, extent, jnp.float32)
    if cuts:
        values = values * shard_levels(own_key, extent, cuts, -0.22, 0.18)
    return jnp.clip(values, -limit, limit).astype(kind)


def setup_inputs(seed: int = 0) -> dict:
    key_list = jax.random.split(jax.random.key(seed), 7)
    integrals = normal_values(key_list[0], (2, V, V, V), V ** -0.5, 0.25, ((1, 8), (2, 4)), jnp.float32)
    doubles = normal_values(key_list[1], (3, V, V), 1.0, 6.0, ((1, 8),), jnp.float32)
    eps_occ = jnp.clip(jax.random.uniform(key_list[2], (NOCC,), jnp.float32, -2.0, -0.5), -2.0, -0.5)
    eps_virt = jnp.clip(jax.random.uniform(key_list[3], (V,), jnp.float32, 0.2, 3.0), 0.2, 3.0)
    triple = jax.random.randint(key_list[4], (3,), 0, NOCC).astype(jnp.int32)
    energy_order = jax.random.permutation(key_list[5], V).astype(jnp.int32)
    return {"integrals": integrals, "doubles": doubles, "eps_occ": eps_occ, "eps_virt": eps_virt, "triple": triple, "energy_order": energy_order}


def reference(integrals, doubles, eps_occ, eps_virt, triple, energy_order):
    highest = lax.Precision.HIGHEST
    k_block = integrals[0]
    i_block = integrals[1]
    first_term = jnp.einsum('bcd,ad->bca', k_block, doubles[0], precision=highest)
    second_term = jnp.einsum('acd,bd->bca', k_block, doubles[1], precision=highest)
    third_term = jnp.einsum('bad,cd->bca', i_block, doubles[2], precision=highest)
    positions = jnp.arange(V, dtype=jnp.int32)
    one_hot = energy_order[:, None] == positions[None, :]
    virt_energy = jnp.sum(jnp.where(one_hot, eps_virt[None, :], jnp.float32(0.0)), axis=1)
    occ_positions = jnp.arange(NOCC, dtype=jnp.int32)
    occ_hot = triple[:, None] == occ_positions[None, :]
    occ_energy = jnp.sum(jnp.where(occ_hot, eps_occ[None, :], jnp.float32(0.0)))
    denominator = occ_energy - virt_energy[:, None, None] - virt_energy[None, :, None] - virt_energy[None, None, :]
    amplitudes = (first_term + second_term + third_term) / denominator
    grad = jnp.einsum('bca,bcd->ad', amplitudes, k_block, precision=highest)
    return amplitudes, grad
```

```python
import functools

import jax
import jax.numpy as jnp
from jax import lax
from jax.experimental import pallas as pl
from jax.experimental.pallas import tpu as pltpu
from jax.sharding import PartitionSpec as P

F32 = jnp.float32
BF16 = jnp.bfloat16
NT = (((1,), (1,)), ((), ()))
NN = (((1,), (0,)), ((), ()))
LANES = 128
WIDE = 256
SHARE = 1000
VMEM_BYTES = 48 * 1024 * 1024


def split(x):
    head = x.astype(BF16)
    return head, (x - head.astype(F32)).astype(BF16)


def dot3(both, right, dims):
    rows = both.shape[0] // 2

    def dot(a, b):
        return lax.dot_general(a, b, dims, preferred_element_type=F32)

    main = dot(both, right[0])
    return main[:rows] + (main[rows:] + dot(both[:rows], right[1]))


def stack(x):
    return jnp.concatenate(split(x), axis=0)


def params(cost_flops, cost_bytes):
    return dict(
        compiler_params=pltpu.CompilerParams(
            dimension_semantics=("arbitrary",), vmem_limit_bytes=VMEM_BYTES
        ),
        cost_estimate=pl.CostEstimate(
            flops=cost_flops // SHARE, bytes_accessed=cost_bytes // SHARE, transcendentals=0
        ),
    )


def second_kernel(peers, tile, per_dot, k_ref, *refs):
    count = (len(refs) - 2) // 2
    d_refs, out_refs = refs[:count], refs[count : 2 * count]
    rows, both = refs[2 * count :]
    nc = k_ref.shape[2]
    depth = k_ref.shape[3]
    width = both.shape[0] // 2
    starts = [sum(d.shape[0] for d in d_refs[:q]) for q in range(count)]

    @pl.when(pl.program_id(0) == 0)
    def _():
        for d_ref, at in zip(d_refs, starts):
            h, t = split(d_ref[...])
            both[at : at + d_ref.shape[0], :] = h
            both[width + at : width + at + d_ref.shape[0], :] = t

    left = both[...]
    for p in range(0, tile, per_dot):
        kk = split(k_ref[0, p : p + per_dot].reshape(per_dot * nc, depth))
        r = dot3(left, kk, NT)
        for s in range(per_dot):
            rows[(p + s) * width : (p + s + 1) * width, :] = r[:, s * nc : (s + 1) * nc]
    for out_ref, at in zip(out_refs, starts):
        nb = out_ref.shape[1]
        for peer in range(peers):
            for b in range(nb):
                from_row = at + peer * nb + b
                out_ref[peer, b, :, :] = rows[pl.ds(from_row, tile, stride=width), :]


def second(integrals, d_rows, peers):
    heights = tuple(d.shape[0] for d in d_rows)
    width = sum(heights)
    na, nc, depth = integrals.shape[1:]
    tile = 8
    per_dot = max(1, WIDE // nc)
    flops = 6 * width * na * nc * depth
    size = 4 * (na * nc * depth + width * na * nc)
    return pl.pallas_call(
        functools.partial(second_kernel, peers, tile, per_dot),
        grid=(na // tile,),
        in_specs=[pl.BlockSpec((1, tile, nc, depth), lambda s: (0, s, 0, 0))]
        + [pl.BlockSpec((h, depth), lambda s: (0, 0)) for h in heights],
        out_specs=[
            pl.BlockSpec((peers, h // peers, tile, nc), lambda s: (0, 0, s, 0)) for h in heights
        ],
        out_shape=[jax.ShapeDtypeStruct((peers, h // peers, na, nc), F32) for h in heights],
        scratch_shapes=[
            pltpu.VMEM((tile * width, nc), F32),
            pltpu.VMEM((2 * width, depth), BF16),
        ],
        name="second",
        **params(flops, size),
    )(integrals, *d_rows)


def third_kernel(i_ref, d_ref, *refs):
    out_refs, (head, tail) = refs[:-2], refs[-2:]
    tile, na, depth = i_ref.shape[1:]
    nc = out_refs[0].shape[2]

    @pl.when(pl.program_id(0) == 0)
    def _():
        h, t = split(d_ref[...].T)
        head[...] = h
        tail[...] = t

    r = dot3(stack(i_ref[0].reshape(tile * na, depth)), (head[...], tail[...]), NN)
    for q, out_ref in enumerate(out_refs):
        out_ref[...] = r[:, q * nc : (q + 1) * nc].reshape(tile, na, nc)


def third(integrals, d_rows, blocks):
    nb, na, depth = integrals.shape[1:]
    total = d_rows.shape[0]
    nc = total // blocks
    tile = 4
    flops = 6 * nb * na * total * depth
    size = 4 * (nb * na * depth + nb * na * total)
    return pl.pallas_call(
        third_kernel,
        grid=(nb // tile,),
        in_specs=[
            pl.BlockSpec((1, tile, na, depth), lambda s: (1, s, 0, 0)),
            pl.BlockSpec((total, depth), lambda s: (0, 0)),
        ],
        out_specs=[pl.BlockSpec((tile, na, nc), lambda s: (s, 0, 0))] * blocks,
        out_shape=[jax.ShapeDtypeStruct((nb, na, nc), F32)] * blocks,
        scratch_shapes=[pltpu.VMEM((depth, total), BF16)] * 2,
        name="third",
        **params(flops, size),
    )(integrals, d_rows)


def first_kernel(per_dot, off_ref, k_ref, d_ref, *refs):
    r_refs = refs[:-2]
    out_ref, both = refs[-2:]
    tile, nc, depth = k_ref.shape[1:]
    na = r_refs[0].shape[1]

    @pl.when(pl.program_id(0) == 0)
    def _():
        both[...] = stack(d_ref[...])

    left = both[...]
    for p in range(0, tile, per_dot):
        kk = split(k_ref[0, p : p + per_dot].reshape(per_dot * nc, depth))
        r = dot3(left, kk, NT)
        for s in range(per_dot):
            out_ref[p + s, :, :] = r[:, s * nc : (s + 1) * nc]
    for q, r_ref in enumerate(r_refs):
        at = pl.ds(pl.multiple_of(off_ref[q], na), na)
        for b in range(tile):
            out_ref[b, at, :] += r_ref[b]


def first(integrals, d_rows, offsets, thirds):
    nb, nc, depth = integrals.shape[1:]
    total = d_rows.shape[0]
    na = thirds[0].shape[1]
    per_dot = max(1, WIDE // nc)
    tile = 2 * per_dot
    flops = 6 * nb * nc * total * depth
    size = 4 * (nb * nc * depth + 2 * nb * nc * total)
    return pl.pallas_call(
        functools.partial(first_kernel, per_dot),
        grid_spec=pltpu.PrefetchScalarGridSpec(
            num_scalar_prefetch=1,
            grid=(nb // tile,),
            in_specs=[
                pl.BlockSpec((1, tile, nc, depth), lambda s, o: (0, s, 0, 0)),
                pl.BlockSpec((total, depth), lambda s, o: (0, 0)),
            ]
            + [pl.BlockSpec((tile, na, nc), lambda s, o: (s, 0, 0)) for _ in thirds],
            out_specs=pl.BlockSpec((tile, total, nc), lambda s, o: (s, 0, 0)),
            scratch_shapes=[pltpu.VMEM((2 * total, depth), BF16)],
        ),
        out_shape=jax.ShapeDtypeStruct((nb, total, nc), F32),
        name="first",
        **params(flops, size),
    )(offsets, integrals, d_rows, *thirds)


def finish_kernel(b0, eb_ref, ec_ref, ea_ref, k_ref, q_ref, t_ref, *refs):
    out_ref, grad_ref = refs[-2:]
    tile, nc, depth = k_ref.shape[1:]
    peers, _, na, _ = t_ref.shape
    step = pl.program_id(0)

    @pl.when(step == 0)
    def _():
        grad_ref[...] = refs[1][...] if len(refs) == 4 else jnp.zeros_like(grad_ref)

    amps = []
    for b in range(tile):
        num = t_ref[:, b].reshape(peers * na, nc) + q_ref[b]
        amp = num / ((eb_ref[b0 + step * tile + b] - ec_ref[...]) - ea_ref[...])
        out_ref[b, :, :] = amp.T
        amps.append(amp)
    left = stack(jnp.concatenate(amps, axis=1))
    kk = split(k_ref[0].reshape(tile * nc, depth))
    r = dot3(left, kk, NN)
    for q in range(grad_ref.shape[0]):
        grad_ref[q] += r[:, q * nc : (q + 1) * nc]


def finish(integrals, base, blocks, eb, ec, ea, b0, given):
    nc, depth = integrals.shape[2:]
    peers, nb, na, _ = blocks.shape
    total = peers * na
    tile = 2 * max(1, WIDE // nc)
    at = b0 // tile
    flops = 6 * nb * nc * total * depth
    size = 4 * (nb * nc * depth + 3 * nb * nc * total)
    return pl.pallas_call(
        functools.partial(finish_kernel, b0),
        grid_spec=pltpu.PrefetchScalarGridSpec(
            num_scalar_prefetch=1,
            grid=(nb // tile,),
            in_specs=[
                pl.BlockSpec((1, nc), lambda s, e: (0, 0)),
                pl.BlockSpec((total, nc), lambda s, e: (0, 0)),
                pl.BlockSpec((1, tile, nc, depth), lambda s, e: (0, s + at, 0, 0)),
                pl.BlockSpec((tile, total, nc), lambda s, e: (s + at, 0, 0)),
                pl.BlockSpec((peers, tile, na, nc), lambda s, e: (0, s, 0, 0)),
            ]
            + [
                pl.BlockSpec(memory_space=pl.ANY),
                pl.BlockSpec((depth // nc, total, nc), lambda s, e: (0, 0, 0)),
            ][: len(given)],
            out_specs=[
                pl.BlockSpec((tile, nc, total), lambda s, e: (s + at, 0, 0)),
                pl.BlockSpec((depth // nc, total, nc), lambda s, e: (0, 0, 0)),
            ],
        ),
        out_shape=[
            jax.ShapeDtypeStruct((base.shape[0], nc, total), F32),
            jax.ShapeDtypeStruct((depth // nc, total, nc), F32),
        ],
        input_output_aliases={6: 0} if given else {},
        name="finish",
        **params(flops, size),
    )(eb, ec, ea, integrals, base, blocks, *given)


def energies(eps_occ, eps_virt, triple, energy_order):
    positions = jnp.arange(eps_virt.shape[0], dtype=jnp.int32)
    one_hot = energy_order[:, None] == positions[None, :]
    virt = jnp.sum(jnp.where(one_hot, eps_virt[None, :], F32(0.0)), axis=1)
    occ_positions = jnp.arange(eps_occ.shape[0], dtype=jnp.int32)
    occ_hot = triple[:, None] == occ_positions[None, :]
    occ = jnp.sum(jnp.where(occ_hot, eps_occ[None, :], F32(0.0)))
    return virt, occ


def tie(value, *after):
    return lax.optimization_barrier((value, after))[0]


def in_blocks(n, m, integrals, doubles, eps_occ, eps_virt, triple, energy_order):
    nb, nc, total = integrals.shape[1:]
    i = lax.axis_index("vb")
    j = lax.axis_index("vc")
    depth = total

    def over_b(x, k):
        return lax.ppermute(x, "vb", [(p, p ^ k) for p in range(n)]) if k else x

    def over_c(x, k):
        return lax.ppermute(x, "vc", [(p, p ^ k) for p in range(m)]) if k else x

    def all_over_b(x):
        return lax.all_to_all(x, "vb", split_axis=0, concat_axis=0, tiled=True)

    def in_order(pieces, place, axis):
        x = jnp.stack(pieces)
        ordered = [
            lax.dynamic_index_in_dim(x, place ^ p, 0, False) for p in range(len(pieces))
        ]
        return jnp.concatenate(ordered, axis=axis)

    lots = [nb // 4, nb - nb // 4 - nb // 8, nb // 8]
    starts = [0, lots[0], lots[0] + lots[1]]

    own = doubles[1][: lots[0]]
    rows = in_order([over_b(own, k) for k in range(n)], i, 0)
    (lot,) = second(integrals, (rows,), n)

    share = depth // m
    part = lax.dynamic_slice_in_dim(tie(doubles, rows), j * share, share, axis=2)
    part = jnp.stack([over_b(part, k) for k in range(0, n, 2)])
    part = jnp.stack([part, over_b(part, 1)], axis=1).reshape((n,) + part.shape[1:])
    part = in_order([part[k] for k in range(n)], i, 1)
    arrived = [all_over_b(tie(lot, part))]
    full = in_order([over_c(part, q) for q in range(m)], j, 2)

    d2 = jnp.concatenate([lax.dynamic_slice_in_dim(full[2], (j ^ q) * nc, nc) for q in range(m)])
    thirds = third(integrals, d2, m)

    by_peer = full[1].reshape(n, nb, depth)
    rows = [
        by_peer[:, at : at + lot].reshape(n * lot, depth)
        for at, lot in zip(starts[1:], lots[1:])
    ]
    made = second(integrals, tie(tuple(rows), *thirds), n)
    thirds = [over_c(x, q) for q, x in enumerate(thirds)]
    made = tie(tuple(made), arrived[0])
    arrived.append(all_over_b(made[0]))

    virt, occ = energies(eps_occ, eps_virt, triple, energy_order)
    eb = occ - lax.dynamic_slice_in_dim(virt, i * nb, nb)
    ec = lax.dynamic_slice_in_dim(virt, j * nc, nc)[None, :]
    ea = jnp.broadcast_to(virt[:, None], (total, nc))
    offsets = jnp.stack([(j ^ q) * nc for q in range(m)]).astype(jnp.int32)
    base = first(integrals, full[0], offsets, thirds)

    given = finish(integrals, base, arrived[0], eb, ec, ea, starts[0], ())
    arrived.append(all_over_b(tie(made[1], arrived[1], given[1])))
    for blocks, at in zip(arrived[1:], starts[1:]):
        given = finish(integrals, base, blocks, eb, ec, ea, at, given)
    amplitudes, grad = given

    step = 1
    while step < m:
        bit = (j // step) % 2
        pairs = grad.reshape(-1, 2, total, nc)
        keep = lax.dynamic_index_in_dim(pairs, bit, 1, False)
        give = lax.dynamic_index_in_dim(pairs, 1 - bit, 1, False)
        grad = keep + over_c(give, step)
        step *= 2
    grad = grad.reshape(total, nc)

    grad = sum(
        over_b(lax.dynamic_slice_in_dim(grad, (i ^ k) * nb, nb), k) for k in range(n)
    )
    return amplitudes, grad


def plain(integrals, doubles, eps_occ, eps_virt, triple, energy_order):
    highest = lax.Precision.HIGHEST
    all_doubles = lax.all_gather(doubles, "vb", axis=1, tiled=True)
    k_block = integrals[0]
    i_block = integrals[1]
    nb, nc = k_block.shape[:2]
    first_term = jnp.einsum("pqd,ad->pqa", k_block, all_doubles[0], precision=highest)
    second_local = jnp.einsum("pqd,bd->bqp", k_block, all_doubles[1], precision=highest)
    second_term = lax.all_to_all(second_local, "vb", split_axis=0, concat_axis=2, tiled=True)
    third_local = jnp.einsum("pqd,cd->pcq", i_block, all_doubles[2], precision=highest)
    third_term = lax.all_to_all(third_local, "vc", split_axis=1, concat_axis=2, tiled=True)
    virt, occ = energies(eps_occ, eps_virt, triple, energy_order)
    eb = lax.dynamic_slice_in_dim(virt, lax.axis_index("vb") * nb, nb)
    ec = lax.dynamic_slice_in_dim(virt, lax.axis_index("vc") * nc, nc)
    low = occ - eb[:, None, None] - ec[None, :, None] - virt[None, None, :]
    amplitudes = (first_term + second_term + third_term) / low
    partial = jnp.einsum("bca,bcd->ad", amplitudes, k_block, precision=highest)
    rows = lax.psum_scatter(partial, "vb", scatter_dimension=0, tiled=True)
    grad = lax.psum_scatter(rows, "vc", scatter_dimension=1, tiled=True)
    return amplitudes, grad


def on_device(n, m, *args):
    nb, nc, total = args[0].shape[1:]
    power = n & (n - 1) == 0 and m & (m - 1) == 0
    fits = nc % LANES == 0 and nb % 32 == 0
    if power and fits:
        return in_blocks(n, m, *args)
    return plain(*args)


def solution(mesh):
    n, m = mesh.shape["vb"], mesh.shape["vc"]
    in_specs = (P(None, "vb", "vc", None), P(None, "vb", None), P(), P(), P(), P())
    out_specs = (P("vb", "vc", None), P("vb", "vc"))
    return jax.shard_map(
        functools.partial(on_device, n, m),
        mesh=mesh,
        in_specs=in_specs,
        out_specs=out_specs,
        check_vma=False,
    )
```

```python
import functools

import jax
import jax.numpy as jnp
from jax import lax
from jax.experimental import pallas as pl
from jax.experimental.pallas import tpu as pltpu
from jax.sharding import PartitionSpec as P

F32 = jnp.float32
BF16 = jnp.bfloat16
NT = (((1,), (1,)), ((), ()))
NN = (((1,), (0,)), ((), ()))
LANES = 128
WIDE = 256
SHARE = 1000
VMEM_BYTES = 48 * 1024 * 1024


def split(x):
    head = x.astype(BF16)
    return head, (x - head.astype(F32)).astype(BF16)


def dot3(both, right, dims):
    rows = both.shape[0] // 2

    def dot(a, b):
        return lax.dot_general(a, b, dims, preferred_element_type=F32)

    main = dot(both, right[0])
    return main[:rows] + (main[rows:] + dot(both[:rows], right[1]))


def stack(x):
    return jnp.concatenate(split(x), axis=0)


def params(cost_flops, cost_bytes):
    return dict(
        compiler_params=pltpu.CompilerParams(
            dimension_semantics=("arbitrary",), vmem_limit_bytes=VMEM_BYTES
        ),
        cost_estimate=pl.CostEstimate(
            flops=cost_flops // SHARE, bytes_accessed=cost_bytes // SHARE, transcendentals=0
        ),
    )


def second_kernel(peers, tile, per_dot, k_ref, *refs):
    count = (len(refs) - 2) // 2
    d_refs, out_refs = refs[:count], refs[count : 2 * count]
    rows, both = refs[2 * count :]
    nc = k_ref.shape[2]
    depth = k_ref.shape[3]
    width = both.shape[0] // 2
    starts = [sum(d.shape[0] for d in d_refs[:q]) for q in range(count)]

    @pl.when(pl.program_id(0) == 0)
    def _():
        for d_ref, at in zip(d_refs, starts):
            h, t = split(d_ref[...])
            both[at : at + d_ref.shape[0], :] = h
            both[width + at : width + at + d_ref.shape[0], :] = t

    left = both[...]
    for p in range(0, tile, per_dot):
        kk = split(k_ref[0, p : p + per_dot].reshape(per_dot * nc, depth))
        r = dot3(left, kk, NT)
        for s in range(per_dot):
            rows[(p + s) * width : (p + s + 1) * width, :] = r[:, s * nc : (s + 1) * nc]
    for out_ref, at in zip(out_refs, starts):
        nb = out_ref.shape[1]
        for peer in range(peers):
            for b in range(nb):
                from_row = at + peer * nb + b
                out_ref[peer, b, :, :] = rows[pl.ds(from_row, tile, stride=width), :]


def second(integrals, d_rows, peers):
    heights = tuple(d.shape[0] for d in d_rows)
    width = sum(heights)
    na, nc, depth = integrals.shape[1:]
    tile = 8
    per_dot = max(1, WIDE // nc)
    flops = 6 * width * na * nc * depth
    size = 4 * (na * nc * depth + width * na * nc)
    return pl.pallas_call(
        functools.partial(second_kernel, peers, tile, per_dot),
        grid=(na // tile,),
        in_specs=[pl.BlockSpec((1, tile, nc, depth), lambda s: (0, s, 0, 0))]
        + [pl.BlockSpec((h, depth), lambda s: (0, 0)) for h in heights],
        out_specs=[
            pl.BlockSpec((peers, h // peers, tile, nc), lambda s: (0, 0, s, 0)) for h in heights
        ],
        out_shape=[pltpu.HBM((peers, h // peers, na, nc), F32) for h in heights],
        scratch_shapes=[
            pltpu.VMEM((tile * width, nc), F32),
            pltpu.VMEM((2 * width, depth), BF16),
        ],
        name="second",
        **params(flops, size),
    )(integrals, *d_rows)


def third_kernel(i_ref, d_ref, *refs):
    out_refs, (head, tail) = refs[:-2], refs[-2:]
    tile, na, depth = i_ref.shape[1:]
    nc = out_refs[0].shape[2]

    @pl.when(pl.program_id(0) == 0)
    def _():
        h, t = split(d_ref[...].T)
        head[...] = h
        tail[...] = t

    r = dot3(stack(i_ref[0].reshape(tile * na, depth)), (head[...], tail[...]), NN)
    for q, out_ref in enumerate(out_refs):
        out_ref[...] = r[:, q * nc : (q + 1) * nc].reshape(tile, na, nc)


def third(integrals, d_rows, blocks):
    nb, na, depth = integrals.shape[1:]
    total = d_rows.shape[0]
    nc = total // blocks
    tile = 4
    flops = 6 * nb * na * total * depth
    size = 4 * (nb * na * depth + nb * na * total)
    return pl.pallas_call(
        third_kernel,
        grid=(nb // tile,),
        in_specs=[
            pl.BlockSpec((1, tile, na, depth), lambda s: (1, s, 0, 0)),
            pl.BlockSpec((total, depth), lambda s: (0, 0)),
        ],
        out_specs=[pl.BlockSpec((tile, na, nc), lambda s: (s, 0, 0))] * blocks,
        out_shape=[pltpu.HBM((nb, na, nc), F32)] * blocks,
        scratch_shapes=[pltpu.VMEM((depth, total), BF16)] * 2,
        name="third",
        **params(flops, size),
    )(integrals, d_rows)


def first_kernel(per_dot, off_ref, k_ref, d_ref, *refs):
    r_refs = refs[:-2]
    out_ref, both = refs[-2:]
    tile, nc, depth = k_ref.shape[1:]
    na = r_refs[0].shape[1]

    @pl.when(pl.program_id(0) == 0)
    def _():
        both[...] = stack(d_ref[...])

    left = both[...]
    for p in range(0, tile, per_dot):
        kk = split(k_ref[0, p : p + per_dot].reshape(per_dot * nc, depth))
        r = dot3(left, kk, NT)
        for s in range(per_dot):
            out_ref[p + s, :, :] = r[:, s * nc : (s + 1) * nc]
    for q, r_ref in enumerate(r_refs):
        at = pl.ds(pl.multiple_of(off_ref[q], na), na)
        for b in range(tile):
            out_ref[b, at, :] += r_ref[b]


def first(integrals, d_rows, offsets, thirds):
    nb, nc, depth = integrals.shape[1:]
    total = d_rows.shape[0]
    na = thirds[0].shape[1]
    per_dot = max(1, WIDE // nc)
    tile = 2 * per_dot
    flops = 6 * nb * nc * total * depth
    size = 4 * (nb * nc * depth + 2 * nb * nc * total)
    return pl.pallas_call(
        functools.partial(first_kernel, per_dot),
        grid_spec=pltpu.PrefetchScalarGridSpec(
            num_scalar_prefetch=1,
            grid=(nb // tile,),
            in_specs=[
                pl.BlockSpec((1, tile, nc, depth), lambda s, o: (0, s, 0, 0)),
                pl.BlockSpec((total, depth), lambda s, o: (0, 0)),
            ]
            + [pl.BlockSpec((tile, na, nc), lambda s, o: (s, 0, 0)) for _ in thirds],
            out_specs=pl.BlockSpec((tile, total, nc), lambda s, o: (s, 0, 0)),
            scratch_shapes=[pltpu.VMEM((2 * total, depth), BF16)],
        ),
        out_shape=pltpu.HBM((nb, total, nc), F32),
        name="first",
        **params(flops, size),
    )(offsets, integrals, d_rows, *thirds)


def finish_kernel(b0, eb_ref, ec_ref, ea_ref, k_ref, q_ref, t_ref, *refs):
    out_ref, grad_ref = refs[-2:]
    tile, nc, depth = k_ref.shape[1:]
    peers, _, na, _ = t_ref.shape
    step = pl.program_id(0)

    @pl.when(step == 0)
    def _():
        grad_ref[...] = refs[1][...] if len(refs) == 4 else jnp.zeros_like(grad_ref)

    amps = []
    for b in range(tile):
        num = t_ref[:, b].reshape(peers * na, nc) + q_ref[b]
        amp = num / ((eb_ref[b0 + step * tile + b] - ec_ref[...]) - ea_ref[...])
        out_ref[b, :, :] = amp.T
        amps.append(amp)
    left = stack(jnp.concatenate(amps, axis=1))
    kk = split(k_ref[0].reshape(tile * nc, depth))
    r = dot3(left, kk, NN)
    for q in range(grad_ref.shape[0]):
        grad_ref[q] += r[:, q * nc : (q + 1) * nc]


def finish(integrals, base, blocks, eb, ec, ea, b0, given):
    nc, depth = integrals.shape[2:]
    peers, nb, na, _ = blocks.shape
    total = peers * na
    tile = 2 * max(1, WIDE // nc)
    at = b0 // tile
    flops = 6 * nb * nc * total * depth
    size = 4 * (nb * nc * depth + 3 * nb * nc * total)
    return pl.pallas_call(
        functools.partial(finish_kernel, b0),
        grid_spec=pltpu.PrefetchScalarGridSpec(
            num_scalar_prefetch=1,
            grid=(nb // tile,),
            in_specs=[
                pl.BlockSpec((1, nc), lambda s, e: (0, 0)),
                pl.BlockSpec((total, nc), lambda s, e: (0, 0)),
                pl.BlockSpec((1, tile, nc, depth), lambda s, e: (0, s + at, 0, 0)),
                pl.BlockSpec((tile, total, nc), lambda s, e: (s + at, 0, 0)),
                pl.BlockSpec((peers, tile, na, nc), lambda s, e: (0, s, 0, 0)),
            ]
            + [
                pl.BlockSpec(memory_space=pl.ANY),
                pl.BlockSpec((depth // nc, total, nc), lambda s, e: (0, 0, 0)),
            ][: len(given)],
            out_specs=[
                pl.BlockSpec((tile, nc, total), lambda s, e: (s + at, 0, 0)),
                pl.BlockSpec((depth // nc, total, nc), lambda s, e: (0, 0, 0)),
            ],
        ),
        out_shape=[
            pltpu.HBM((base.shape[0], nc, total), F32),
            pltpu.HBM((depth // nc, total, nc), F32),
        ],
        input_output_aliases={6: 0} if given else {},
        name="finish",
        **params(flops, size),
    )(eb, ec, ea, integrals, base, blocks, *given)


def energies(eps_occ, eps_virt, triple, energy_order):
    positions = jnp.arange(eps_virt.shape[0], dtype=jnp.int32)
    one_hot = energy_order[:, None] == positions[None, :]
    virt = jnp.sum(jnp.where(one_hot, eps_virt[None, :], F32(0.0)), axis=1)
    occ_positions = jnp.arange(eps_occ.shape[0], dtype=jnp.int32)
    occ_hot = triple[:, None] == occ_positions[None, :]
    occ = jnp.sum(jnp.where(occ_hot, eps_occ[None, :], F32(0.0)))
    return virt, occ


def tie(value, *after):
    return lax.optimization_barrier((value, after))[0]


def in_blocks(n, m, integrals, doubles, eps_occ, eps_virt, triple, energy_order):
    nb, nc, total = integrals.shape[1:]
    i = lax.axis_index("vb")
    j = lax.axis_index("vc")
    depth = total

    def over_b(x, k):
        return lax.ppermute(x, "vb", [(p, p ^ k) for p in range(n)]) if k else x

    def over_c(x, k):
        return lax.ppermute(x, "vc", [(p, p ^ k) for p in range(m)]) if k else x

    def all_over_b(x):
        return lax.all_to_all(x, "vb", split_axis=0, concat_axis=0, tiled=True)

    def in_order(pieces, place, axis):
        x = jnp.stack(pieces)
        ordered = [
            lax.dynamic_index_in_dim(x, place ^ p, 0, False) for p in range(len(pieces))
        ]
        return jnp.concatenate(ordered, axis=axis)

    few = max(nb // 16, 4)
    lots = [nb // 4, nb - nb // 4 - few, few]
    starts = [0, lots[0], lots[0] + lots[1]]

    share = depth // m
    own = doubles[1][: lots[0]]
    own = jnp.concatenate([own[:, q * share : (q + 1) * share] for q in range(m)])
    part = lax.dynamic_slice_in_dim(doubles, j * share, share, axis=2)
    head = jnp.concatenate([own, part.reshape(3 * nb, share)])
    head = jnp.stack([over_b(head, k) for k in range(0, n, 2)])

    def from_last_bit(x):
        x = jnp.stack([x, over_b(x, 1)], axis=1)
        x = x.reshape((n,) + x.shape[2:])
        return jnp.stack([lax.dynamic_index_in_dim(x, i ^ p, 0, False) for p in range(n)])

    rows = from_last_bit(head[:, : m * lots[0]]).reshape(n, m, lots[0], share)
    rows = jnp.concatenate([rows[:, q] for q in range(m)], axis=2).reshape(n * lots[0], depth)
    part = from_last_bit(tie(head[:, m * lots[0] :], rows))
    (lot,) = second(integrals, (rows,), n)
    part, lot = lax.optimization_barrier((part, lot))
    arrived = [all_over_b(lot)]

    part = part.reshape(n, 3, nb, share).transpose(1, 0, 2, 3).reshape(3, total, share)
    step, bits = m // 2, 0
    while step:
        part = jnp.stack([part, over_c(part, step)], axis=bits)
        step, bits = step // 2, bits + 1
    part = part.reshape((m,) + part.shape[bits:])
    full = in_order([part[q] for q in range(m)], j, 2)

    d2 = jnp.concatenate([lax.dynamic_slice_in_dim(full[2], (j ^ q) * nc, nc) for q in range(m)])
    thirds = third(integrals, d2, m)

    by_peer = full[1].reshape(n, nb, depth)
    rows = [
        by_peer[:, at : at + lot].reshape(n * lot, depth)
        for at, lot in zip(starts[1:], lots[1:])
    ]
    made = second(integrals, tie(tuple(rows), *thirds), n)
    thirds = [over_c(x, q) for q, x in enumerate(thirds)]
    made = tie(tuple(made), arrived[0])
    arrived.append(all_over_b(made[0]))

    virt, occ = energies(eps_occ, eps_virt, triple, energy_order)
    eb = occ - lax.dynamic_slice_in_dim(virt, i * nb, nb)
    ec = lax.dynamic_slice_in_dim(virt, j * nc, nc)[None, :]
    ea = jnp.broadcast_to(virt[:, None], (total, nc))
    offsets = jnp.stack([(j ^ q) * nc for q in range(m)]).astype(jnp.int32)
    base = first(integrals, full[0], offsets, thirds)

    given = finish(integrals, base, arrived[0], eb, ec, ea, starts[0], ())
    arrived.append(all_over_b(tie(made[1], arrived[1], given[1])))
    for blocks, at in zip(arrived[1:], starts[1:]):
        given = finish(integrals, base, blocks, eb, ec, ea, at, given)
    amplitudes, grad = given

    step = 1
    while step < m:
        bit = (j // step) % 2
        pairs = grad.reshape(-1, 2, total, nc)
        keep = lax.dynamic_index_in_dim(pairs, bit, 1, False)
        give = lax.dynamic_index_in_dim(pairs, 1 - bit, 1, False)
        grad = keep + over_c(give, step)
        step *= 2
    grad = grad.reshape(total, nc)

    grad = jnp.sum(all_over_b(grad.reshape(n, nb, nc)), axis=0)
    return amplitudes, grad


def plain(integrals, doubles, eps_occ, eps_virt, triple, energy_order):
    highest = lax.Precision.HIGHEST
    all_doubles = lax.all_gather(doubles, "vb", axis=1, tiled=True)
    k_block = integrals[0]
    i_block = integrals[1]
    nb, nc = k_block.shape[:2]
    first_term = jnp.einsum("pqd,ad->pqa", k_block, all_doubles[0], precision=highest)
    second_local = jnp.einsum("pqd,bd->bqp", k_block, all_doubles[1], precision=highest)
    second_term = lax.all_to_all(second_local, "vb", split_axis=0, concat_axis=2, tiled=True)
    third_local = jnp.einsum("pqd,cd->pcq", i_block, all_doubles[2], precision=highest)
    third_term = lax.all_to_all(third_local, "vc", split_axis=1, concat_axis=2, tiled=True)
    virt, occ = energies(eps_occ, eps_virt, triple, energy_order)
    eb = lax.dynamic_slice_in_dim(virt, lax.axis_index("vb") * nb, nb)
    ec = lax.dynamic_slice_in_dim(virt, lax.axis_index("vc") * nc, nc)
    low = occ - eb[:, None, None] - ec[None, :, None] - virt[None, None, :]
    amplitudes = (first_term + second_term + third_term) / low
    partial = jnp.einsum("bca,bcd->ad", amplitudes, k_block, precision=highest)
    rows = lax.psum_scatter(partial, "vb", scatter_dimension=0, tiled=True)
    grad = lax.psum_scatter(rows, "vc", scatter_dimension=1, tiled=True)
    return amplitudes, grad


def on_device(n, m, *args):
    nb, nc, total = args[0].shape[1:]
    power = n & (n - 1) == 0 and m & (m - 1) == 0
    fits = nc % LANES == 0 and nb % 32 == 0
    if power and fits:
        return in_blocks(n, m, *args)
    return plain(*args)


def solution(mesh):
    n, m = mesh.shape["vb"], mesh.shape["vc"]
    in_specs = (P(None, "vb", "vc", None), P(None, "vb", None), P(), P(), P(), P())
    out_specs = (P("vb", "vc", None), P("vb", "vc"))
    return jax.shard_map(
        functools.partial(on_device, n, m),
        mesh=mesh,
        in_specs=in_specs,
        out_specs=out_specs,
        check_vma=False,
    )
```

```python
import functools

import jax
import jax.numpy as jnp
from jax import lax
from jax.experimental import pallas as pl
from jax.experimental.pallas import tpu as pltpu
from jax.sharding import PartitionSpec as P

F32 = jnp.float32
BF16 = jnp.bfloat16
NT = (((1,), (1,)), ((), ()))
NN = (((1,), (0,)), ((), ()))
LANES = 128
WIDE = 256
SHARE = 1000
VMEM_BYTES = 48 * 1024 * 1024


def split(x):
    head = x.astype(BF16)
    return head, (x - head.astype(F32)).astype(BF16)


def dot3(both, right, dims):
    rows = both.shape[0] // 2

    def dot(a, b):
        return lax.dot_general(a, b, dims, preferred_element_type=F32)

    main = dot(both, right[0])
    return main[:rows] + (main[rows:] + dot(both[:rows], right[1]))


def stack(x):
    return jnp.concatenate(split(x), axis=0)


def params(cost_flops, cost_bytes):
    return dict(
        compiler_params=pltpu.CompilerParams(
            dimension_semantics=("arbitrary",), vmem_limit_bytes=VMEM_BYTES
        ),
        cost_estimate=pl.CostEstimate(
            flops=cost_flops // SHARE, bytes_accessed=cost_bytes // SHARE, transcendentals=0
        ),
    )


def second_kernel(peers, count, tile, per_dot, k_ref, *refs):
    d_refs, out_refs = refs[:count], refs[-2 - count : -2]
    rows, both = refs[-2:]
    nc = k_ref.shape[2]
    depth = k_ref.shape[3]
    width = both.shape[0] // 2
    starts = [sum(d.shape[0] for d in d_refs[:q]) for q in range(count)]

    @pl.when(pl.program_id(0) == 0)
    def _():
        for d_ref, at in zip(d_refs, starts):
            h, t = split(d_ref[...])
            both[at : at + d_ref.shape[0], :] = h
            both[width + at : width + at + d_ref.shape[0], :] = t

    left = both[...]
    for p in range(0, tile, per_dot):
        kk = split(k_ref[0, p : p + per_dot].reshape(per_dot * nc, depth))
        r = dot3(left, kk, NT)
        for s in range(per_dot):
            rows[(p + s) * width : (p + s + 1) * width, :] = r[:, s * nc : (s + 1) * nc]
    for out_ref, at in zip(out_refs, starts):
        nb = out_ref.shape[1]
        for peer in range(peers):
            for b in range(nb):
                from_row = at + peer * nb + b
                out_ref[peer, b, :, :] = rows[pl.ds(from_row, tile, stride=width), :]


def second(integrals, d_rows, peers, a0, count_a, into=()):
    heights = tuple(d.shape[0] for d in d_rows)
    width = sum(heights)
    na, nc, depth = integrals.shape[1:]
    tile = 8
    per_dot = max(1, WIDE // nc)
    flops = 6 * width * count_a * nc * depth
    size = 4 * (count_a * nc * depth + width * count_a * nc)
    at = a0 // tile
    count = len(d_rows)
    return pl.pallas_call(
        functools.partial(second_kernel, peers, count, tile, per_dot),
        grid=(count_a // tile,),
        in_specs=[pl.BlockSpec((1, tile, nc, depth), lambda s: (0, s + at, 0, 0))]
        + [pl.BlockSpec((h, depth), lambda s: (0, 0)) for h in heights]
        + [pl.BlockSpec(memory_space=pl.ANY) for _ in into],
        out_specs=[
            pl.BlockSpec((peers, h // peers, tile, nc), lambda s: (0, 0, s + at, 0))
            for h in heights
        ],
        input_output_aliases={1 + count + q: q for q in range(len(into))},
        out_shape=[pltpu.HBM((peers, h // peers, na, nc), F32) for h in heights],
        scratch_shapes=[
            pltpu.VMEM((tile * width, nc), F32),
            pltpu.VMEM((2 * width, depth), BF16),
        ],
        name="second",
        **params(flops, size),
    )(integrals, *d_rows, *into)


def third_kernel(i_ref, d_ref, *refs):
    out_refs, (head, tail) = refs[:-2], refs[-2:]
    tile, na, depth = i_ref.shape[1:]
    nc = out_refs[0].shape[2]

    @pl.when(pl.program_id(0) == 0)
    def _():
        h, t = split(d_ref[...].T)
        head[...] = h
        tail[...] = t

    r = dot3(stack(i_ref[0].reshape(tile * na, depth)), (head[...], tail[...]), NN)
    for q, out_ref in enumerate(out_refs):
        out_ref[...] = r[:, q * nc : (q + 1) * nc].reshape(tile, na, nc)


def third(integrals, d_rows, blocks):
    nb, na, depth = integrals.shape[1:]
    total = d_rows.shape[0]
    nc = total // blocks
    tile = 4
    flops = 6 * nb * na * total * depth
    size = 4 * (nb * na * depth + nb * na * total)
    return pl.pallas_call(
        third_kernel,
        grid=(nb // tile,),
        in_specs=[
            pl.BlockSpec((1, tile, na, depth), lambda s: (1, s, 0, 0)),
            pl.BlockSpec((total, depth), lambda s: (0, 0)),
        ],
        out_specs=[pl.BlockSpec((tile, na, nc), lambda s: (s, 0, 0))] * blocks,
        out_shape=[pltpu.HBM((nb, na, nc), F32)] * blocks,
        scratch_shapes=[pltpu.VMEM((depth, total), BF16)] * 2,
        name="third",
        **params(flops, size),
    )(integrals, d_rows)


def first_kernel(per_dot, off_ref, k_ref, d_ref, *refs):
    r_refs = refs[:-2]
    out_ref, both = refs[-2:]
    tile, nc, depth = k_ref.shape[1:]
    na = r_refs[0].shape[1]

    @pl.when(pl.program_id(0) == 0)
    def _():
        both[...] = stack(d_ref[...])

    left = both[...]
    for p in range(0, tile, per_dot):
        kk = split(k_ref[0, p : p + per_dot].reshape(per_dot * nc, depth))
        r = dot3(left, kk, NT)
        for s in range(per_dot):
            out_ref[p + s, :, :] = r[:, s * nc : (s + 1) * nc]
    for q, r_ref in enumerate(r_refs):
        at = pl.ds(pl.multiple_of(off_ref[q], na), na)
        for b in range(tile):
            out_ref[b, at, :] += r_ref[b]


def first(integrals, d_rows, offsets, thirds):
    nb, nc, depth = integrals.shape[1:]
    total = d_rows.shape[0]
    na = thirds[0].shape[1]
    per_dot = max(1, WIDE // nc)
    tile = 2 * per_dot
    flops = 6 * nb * nc * total * depth
    size = 4 * (nb * nc * depth + 2 * nb * nc * total)
    return pl.pallas_call(
        functools.partial(first_kernel, per_dot),
        grid_spec=pltpu.PrefetchScalarGridSpec(
            num_scalar_prefetch=1,
            grid=(nb // tile,),
            in_specs=[
                pl.BlockSpec((1, tile, nc, depth), lambda s, o: (0, s, 0, 0)),
                pl.BlockSpec((total, depth), lambda s, o: (0, 0)),
            ]
            + [pl.BlockSpec((tile, na, nc), lambda s, o: (s, 0, 0)) for _ in thirds],
            out_specs=pl.BlockSpec((tile, total, nc), lambda s, o: (s, 0, 0)),
            scratch_shapes=[pltpu.VMEM((2 * total, depth), BF16)],
        ),
        out_shape=pltpu.HBM((nb, total, nc), F32),
        name="first",
        **params(flops, size),
    )(offsets, integrals, d_rows, *thirds)


def finish_kernel(b0, eb_ref, ec_ref, ea_ref, k_ref, q_ref, t_ref, *refs):
    out_ref, grad_ref = refs[-2:]
    tile, nc, depth = k_ref.shape[1:]
    peers, _, na, _ = t_ref.shape
    step = pl.program_id(0)

    @pl.when(step == 0)
    def _():
        grad_ref[...] = refs[1][...] if len(refs) == 4 else jnp.zeros_like(grad_ref)

    amps = []
    for b in range(tile):
        num = t_ref[:, b].reshape(peers * na, nc) + q_ref[b]
        amp = num / ((eb_ref[b0 + step * tile + b] - ec_ref[...]) - ea_ref[...])
        out_ref[b, :, :] = amp.T
        amps.append(amp)
    left = stack(jnp.concatenate(amps, axis=1))
    kk = split(k_ref[0].reshape(tile * nc, depth))
    r = dot3(left, kk, NN)
    for q in range(grad_ref.shape[0]):
        grad_ref[q] += r[:, q * nc : (q + 1) * nc]


def finish(integrals, base, blocks, eb, ec, ea, b0, given):
    nc, depth = integrals.shape[2:]
    peers, nb, na, _ = blocks.shape
    total = peers * na
    tile = 2 * max(1, WIDE // nc)
    at = b0 // tile
    flops = 6 * nb * nc * total * depth
    size = 4 * (nb * nc * depth + 3 * nb * nc * total)
    return pl.pallas_call(
        functools.partial(finish_kernel, b0),
        grid_spec=pltpu.PrefetchScalarGridSpec(
            num_scalar_prefetch=1,
            grid=(nb // tile,),
            in_specs=[
                pl.BlockSpec((1, nc), lambda s, e: (0, 0)),
                pl.BlockSpec((total, nc), lambda s, e: (0, 0)),
                pl.BlockSpec((1, tile, nc, depth), lambda s, e: (0, s + at, 0, 0)),
                pl.BlockSpec((tile, total, nc), lambda s, e: (s + at, 0, 0)),
                pl.BlockSpec((peers, tile, na, nc), lambda s, e: (0, s, 0, 0)),
            ]
            + [
                pl.BlockSpec(memory_space=pl.ANY),
                pl.BlockSpec((depth // nc, total, nc), lambda s, e: (0, 0, 0)),
            ][: len(given)],
            out_specs=[
                pl.BlockSpec((tile, nc, total), lambda s, e: (s + at, 0, 0)),
                pl.BlockSpec((depth // nc, total, nc), lambda s, e: (0, 0, 0)),
            ],
        ),
        out_shape=[
            pltpu.HBM((base.shape[0], nc, total), F32),
            pltpu.HBM((depth // nc, total, nc), F32),
        ],
        input_output_aliases={6: 0, 7: 1} if given else {},
        name="finish",
        **params(flops, size),
    )(eb, ec, ea, integrals, base, blocks, *given)


def energies(eps_occ, eps_virt, triple, energy_order):
    positions = jnp.arange(eps_virt.shape[0], dtype=jnp.int32)
    one_hot = energy_order[:, None] == positions[None, :]
    virt = jnp.sum(jnp.where(one_hot, eps_virt[None, :], F32(0.0)), axis=1)
    occ_positions = jnp.arange(eps_occ.shape[0], dtype=jnp.int32)
    occ_hot = triple[:, None] == occ_positions[None, :]
    occ = jnp.sum(jnp.where(occ_hot, eps_occ[None, :], F32(0.0)))
    return virt, occ


def tie(value, *after):
    return lax.optimization_barrier((value, after))[0]


def in_blocks(n, m, integrals, doubles, eps_occ, eps_virt, triple, energy_order):
    nb, nc, total = integrals.shape[1:]
    i = lax.axis_index("vb")
    j = lax.axis_index("vc")
    depth = total

    def over_b(x, k):
        return lax.ppermute(x, "vb", [(p, p ^ k) for p in range(n)]) if k else x

    def over_c(x, k):
        return lax.ppermute(x, "vc", [(p, p ^ k) for p in range(m)]) if k else x

    def all_over_b(x):
        return lax.all_to_all(x, "vb", split_axis=0, concat_axis=0, tiled=True)

    def in_order(pieces, place, axis):
        x = jnp.stack(pieces)
        ordered = [
            lax.dynamic_index_in_dim(x, place ^ p, 0, False) for p in range(len(pieces))
        ]
        return jnp.concatenate(ordered, axis=axis)

    few = max(nb // 16, 4)
    lots = [nb // 4, nb - nb // 4 - few, few]
    starts = [0, lots[0], lots[0] + lots[1]]

    share = depth // m
    own = doubles[1][: lots[0]]
    part = lax.dynamic_slice_in_dim(doubles, j * share, share, axis=2)
    far_rows = jnp.stack([over_b(own, k) for k in range(0, n, 2)])
    far_part = jnp.stack([over_b(part, k) for k in range(0, n, 2)])

    def from_last_bit(x):
        x = jnp.stack([x, over_b(x, 1)], axis=1)
        x = x.reshape((n,) + x.shape[2:])
        return jnp.stack([lax.dynamic_index_in_dim(x, i ^ p, 0, False) for p in range(n)])

    rows = from_last_bit(far_rows).reshape(n * lots[0], depth)
    half = nb // 2
    begun = second(integrals, (rows,), n, 0, half)
    far_part, begun = lax.optimization_barrier((far_part, tuple(begun)))
    part = from_last_bit(far_part)
    (lot,) = second(integrals, (rows,), n, half, nb - half, begun)
    part, lot = lax.optimization_barrier((part, lot))
    arrived = [all_over_b(lot)]

    part = part.reshape(n, 3, nb, share).transpose(1, 0, 2, 3).reshape(3, total, share)
    step, bits = m // 2, 0
    while step:
        part = jnp.stack([part, over_c(part, step)], axis=bits)
        step, bits = step // 2, bits + 1
    part = part.reshape((m,) + part.shape[bits:])
    full = in_order([part[q] for q in range(m)], j, 2)

    d2 = jnp.concatenate([lax.dynamic_slice_in_dim(full[2], (j ^ q) * nc, nc) for q in range(m)])
    thirds = third(integrals, d2, m)

    by_peer = full[1].reshape(n, nb, depth)
    rows = [
        by_peer[:, at : at + lot].reshape(n * lot, depth)
        for at, lot in zip(starts[1:], lots[1:])
    ]
    made = second(integrals, tie(tuple(rows), *thirds), n, 0, nb)
    thirds = [over_c(x, q) for q, x in enumerate(thirds)]
    made = tie(tuple(made), arrived[0])
    arrived.append(all_over_b(made[0]))

    virt, occ = energies(eps_occ, eps_virt, triple, energy_order)
    eb = occ - lax.dynamic_slice_in_dim(virt, i * nb, nb)
    ec = lax.dynamic_slice_in_dim(virt, j * nc, nc)[None, :]
    ea = jnp.broadcast_to(virt[:, None], (total, nc))
    offsets = jnp.stack([(j ^ q) * nc for q in range(m)]).astype(jnp.int32)
    base = first(integrals, full[0], offsets, thirds)

    given = finish(integrals, base, arrived[0], eb, ec, ea, starts[0], ())
    arrived.append(all_over_b(tie(made[1], arrived[1], given[1])))
    for blocks, at in zip(arrived[1:], starts[1:]):
        given = finish(integrals, base, blocks, eb, ec, ea, at, given)
    amplitudes, grad = given

    step = 1
    while step < m:
        bit = (j // step) % 2
        pairs = grad.reshape(-1, 2, total, nc)
        keep = lax.dynamic_index_in_dim(pairs, bit, 1, False)
        give = lax.dynamic_index_in_dim(pairs, 1 - bit, 1, False)
        grad = keep + over_c(give, step)
        step *= 2
    grad = grad.reshape(total, nc)

    grad = jnp.sum(all_over_b(grad.reshape(n, nb, nc)), axis=0)
    return amplitudes, grad


def plain(integrals, doubles, eps_occ, eps_virt, triple, energy_order):
    highest = lax.Precision.HIGHEST
    all_doubles = lax.all_gather(doubles, "vb", axis=1, tiled=True)
    k_block = integrals[0]
    i_block = integrals[1]
    nb, nc = k_block.shape[:2]
    first_term = jnp.einsum("pqd,ad->pqa", k_block, all_doubles[0], precision=highest)
    second_local = jnp.einsum("pqd,bd->bqp", k_block, all_doubles[1], precision=highest)
    second_term = lax.all_to_all(second_local, "vb", split_axis=0, concat_axis=2, tiled=True)
    third_local = jnp.einsum("pqd,cd->pcq", i_block, all_doubles[2], precision=highest)
    third_term = lax.all_to_all(third_local, "vc", split_axis=1, concat_axis=2, tiled=True)
    virt, occ = energies(eps_occ, eps_virt, triple, energy_order)
    eb = lax.dynamic_slice_in_dim(virt, lax.axis_index("vb") * nb, nb)
    ec = lax.dynamic_slice_in_dim(virt, lax.axis_index("vc") * nc, nc)
    low = occ - eb[:, None, None] - ec[None, :, None] - virt[None, None, :]
    amplitudes = (first_term + second_term + third_term) / low
    partial = jnp.einsum("bca,bcd->ad", amplitudes, k_block, precision=highest)
    rows = lax.psum_scatter(partial, "vb", scatter_dimension=0, tiled=True)
    grad = lax.psum_scatter(rows, "vc", scatter_dimension=1, tiled=True)
    return amplitudes, grad


def on_device(n, m, *args):
    nb, nc, total = args[0].shape[1:]
    power = n & (n - 1) == 0 and m & (m - 1) == 0
    fits = nc % LANES == 0 and nb % 32 == 0
    if power and fits:
        return in_blocks(n, m, *args)
    return plain(*args)


def solution(mesh):
    n, m = mesh.shape["vb"], mesh.shape["vc"]
    in_specs = (P(None, "vb", "vc", None), P(None, "vb", None), P(), P(), P(), P())
    out_specs = (P("vb", "vc", None), P("vb", "vc"))
    return jax.shard_map(
        functools.partial(on_device, n, m),
        mesh=mesh,
        in_specs=in_specs,
        out_specs=out_specs,
        check_vma=False,
    )
```

```python
import functools

import jax
import jax.numpy as jnp
from jax import lax
from jax.experimental import pallas as pl
from jax.experimental.pallas import tpu as pltpu
from jax.sharding import PartitionSpec as P

F32 = jnp.float32
BF16 = jnp.bfloat16
NT = (((1,), (1,)), ((), ()))
NN = (((1,), (0,)), ((), ()))
LANES = 128
WIDE = 256
SHARE = 1000
VMEM_BYTES = 48 * 1024 * 1024


def split(x):
    head = x.astype(BF16)
    return head, (x - head.astype(F32)).astype(BF16)


def dot3(both, right, dims):
    rows = both.shape[0] // 2

    def dot(a, b):
        return lax.dot_general(a, b, dims, preferred_element_type=F32)

    main = dot(both, right[0])
    return main[:rows] + (main[rows:] + dot(both[:rows], right[1]))


def stack(x):
    return jnp.concatenate(split(x), axis=0)


def params(cost_flops, cost_bytes):
    return dict(
        compiler_params=pltpu.CompilerParams(
            dimension_semantics=("arbitrary",), vmem_limit_bytes=VMEM_BYTES
        ),
        cost_estimate=pl.CostEstimate(
            flops=cost_flops // SHARE, bytes_accessed=cost_bytes // SHARE, transcendentals=0
        ),
    )


def second_kernel(peers, count, tile, per_dot, k_ref, *refs):
    d_refs, out_refs = refs[:count], refs[-2 - count : -2]
    rows, both = refs[-2:]
    nc = k_ref.shape[2]
    depth = k_ref.shape[3]
    width = both.shape[0] // 2
    starts = [sum(d.shape[0] for d in d_refs[:q]) for q in range(count)]

    @pl.when(pl.program_id(0) == 0)
    def _():
        for d_ref, at in zip(d_refs, starts):
            h, t = split(d_ref[...])
            both[at : at + d_ref.shape[0], :] = h
            both[width + at : width + at + d_ref.shape[0], :] = t

    left = both[...]
    for p in range(0, tile, per_dot):
        kk = split(k_ref[0, p : p + per_dot].reshape(per_dot * nc, depth))
        r = dot3(left, kk, NT)
        for s in range(per_dot):
            rows[(p + s) * width : (p + s + 1) * width, :] = r[:, s * nc : (s + 1) * nc]
    for out_ref, at in zip(out_refs, starts):
        nb = out_ref.shape[1]
        for peer in range(peers):
            for b in range(nb):
                from_row = at + peer * nb + b
                out_ref[peer, b, :, :] = rows[pl.ds(from_row, tile, stride=width), :]


def second(integrals, d_rows, peers, a0, count_a, into=()):
    heights = tuple(d.shape[0] for d in d_rows)
    width = sum(heights)
    na, nc, depth = integrals.shape[1:]
    tile = 8
    per_dot = max(1, WIDE // nc)
    flops = 6 * width * count_a * nc * depth
    size = 4 * (count_a * nc * depth + width * count_a * nc)
    at = a0 // tile
    count = len(d_rows)
    return pl.pallas_call(
        functools.partial(second_kernel, peers, count, tile, per_dot),
        grid=(count_a // tile,),
        in_specs=[pl.BlockSpec((1, tile, nc, depth), lambda s: (0, s + at, 0, 0))]
        + [pl.BlockSpec((h, depth), lambda s: (0, 0)) for h in heights]
        + [pl.BlockSpec(memory_space=pl.ANY) for _ in into],
        out_specs=[
            pl.BlockSpec((peers, h // peers, tile, nc), lambda s: (0, 0, s + at, 0))
            for h in heights
        ],
        input_output_aliases={1 + count + q: q for q in range(len(into))},
        out_shape=[pltpu.HBM((peers, h // peers, na, nc), F32) for h in heights],
        scratch_shapes=[
            pltpu.VMEM((tile * width, nc), F32),
            pltpu.VMEM((2 * width, depth), BF16),
        ],
        name="second",
        **params(flops, size),
    )(integrals, *d_rows, *into)


def third_kernel(i_ref, d_ref, *refs):
    out_refs, (head, tail) = refs[:-2], refs[-2:]
    tile, na, depth = i_ref.shape[1:]
    nc = out_refs[0].shape[2]

    @pl.when(pl.program_id(0) == 0)
    def _():
        h, t = split(d_ref[...].T)
        head[...] = h
        tail[...] = t

    r = dot3(stack(i_ref[0].reshape(tile * na, depth)), (head[...], tail[...]), NN)
    for q, out_ref in enumerate(out_refs):
        out_ref[...] = r[:, q * nc : (q + 1) * nc].reshape(tile, na, nc)


def third(integrals, d_rows, blocks):
    nb, na, depth = integrals.shape[1:]
    total = d_rows.shape[0]
    nc = total // blocks
    tile = 4
    flops = 6 * nb * na * total * depth
    size = 4 * (nb * na * depth + nb * na * total)
    return pl.pallas_call(
        third_kernel,
        grid=(nb // tile,),
        in_specs=[
            pl.BlockSpec((1, tile, na, depth), lambda s: (1, s, 0, 0)),
            pl.BlockSpec((total, depth), lambda s: (0, 0)),
        ],
        out_specs=[pl.BlockSpec((tile, na, nc), lambda s: (s, 0, 0))] * blocks,
        out_shape=[pltpu.HBM((nb, na, nc), F32)] * blocks,
        scratch_shapes=[pltpu.VMEM((depth, total), BF16)] * 2,
        name="third",
        **params(flops, size),
    )(integrals, d_rows)


def first_kernel(per_dot, off_ref, k_ref, d_ref, *refs):
    r_refs = refs[:-2]
    out_ref, both = refs[-2:]
    tile, nc, depth = k_ref.shape[1:]
    na = r_refs[0].shape[1]

    @pl.when(pl.program_id(0) == 0)
    def _():
        both[...] = stack(d_ref[...])

    left = both[...]
    for p in range(0, tile, per_dot):
        kk = split(k_ref[0, p : p + per_dot].reshape(per_dot * nc, depth))
        r = dot3(left, kk, NT)
        for s in range(per_dot):
            out_ref[p + s, :, :] = r[:, s * nc : (s + 1) * nc]
    for q, r_ref in enumerate(r_refs):
        at = pl.ds(pl.multiple_of(off_ref[q], na), na)
        for b in range(tile):
            out_ref[b, at, :] += r_ref[b]


def first(integrals, d_rows, offsets, thirds):
    nb, nc, depth = integrals.shape[1:]
    total = d_rows.shape[0]
    na = thirds[0].shape[1]
    per_dot = max(1, WIDE // nc)
    tile = 2 * per_dot
    flops = 6 * nb * nc * total * depth
    size = 4 * (nb * nc * depth + 2 * nb * nc * total)
    return pl.pallas_call(
        functools.partial(first_kernel, per_dot),
        grid_spec=pltpu.PrefetchScalarGridSpec(
            num_scalar_prefetch=1,
            grid=(nb // tile,),
            in_specs=[
                pl.BlockSpec((1, tile, nc, depth), lambda s, o: (0, s, 0, 0)),
                pl.BlockSpec((total, depth), lambda s, o: (0, 0)),
            ]
            + [pl.BlockSpec((tile, na, nc), lambda s, o: (s, 0, 0)) for _ in thirds],
            out_specs=pl.BlockSpec((tile, total, nc), lambda s, o: (s, 0, 0)),
            scratch_shapes=[pltpu.VMEM((2 * total, depth), BF16)],
        ),
        out_shape=pltpu.HBM((nb, total, nc), F32),
        name="first",
        **params(flops, size),
    )(offsets, integrals, d_rows, *thirds)


def finish_kernel(b0, eb_ref, ec_ref, ea_ref, k_ref, q_ref, t_ref, *refs):
    out_ref, grad_ref = refs[-2:]
    tile, nc, depth = k_ref.shape[1:]
    peers, _, na, _ = t_ref.shape
    step = pl.program_id(0)

    @pl.when(step == 0)
    def _():
        grad_ref[...] = refs[1][...] if len(refs) == 4 else jnp.zeros_like(grad_ref)

    amps = []
    for b in range(tile):
        num = t_ref[:, b].reshape(peers * na, nc) + q_ref[b]
        amp = num / ((eb_ref[b0 + step * tile + b] - ec_ref[...]) - ea_ref[...])
        out_ref[b, :, :] = amp.T
        amps.append(amp)
    left = stack(jnp.concatenate(amps, axis=1))
    kk = split(k_ref[0].reshape(tile * nc, depth))
    r = dot3(left, kk, NN)
    for q in range(grad_ref.shape[0]):
        grad_ref[q] += r[:, q * nc : (q + 1) * nc]


def finish(integrals, base, blocks, eb, ec, ea, b0, given):
    nc, depth = integrals.shape[2:]
    peers, nb, na, _ = blocks.shape
    total = peers * na
    tile = 2 * max(1, WIDE // nc)
    at = b0 // tile
    flops = 6 * nb * nc * total * depth
    size = 4 * (nb * nc * depth + 3 * nb * nc * total)
    return pl.pallas_call(
        functools.partial(finish_kernel, b0),
        grid_spec=pltpu.PrefetchScalarGridSpec(
            num_scalar_prefetch=1,
            grid=(nb // tile,),
            in_specs=[
                pl.BlockSpec((1, nc), lambda s, e: (0, 0)),
                pl.BlockSpec((total, nc), lambda s, e: (0, 0)),
                pl.BlockSpec((1, tile, nc, depth), lambda s, e: (0, s + at, 0, 0)),
                pl.BlockSpec((tile, total, nc), lambda s, e: (s + at, 0, 0)),
                pl.BlockSpec((peers, tile, na, nc), lambda s, e: (0, s, 0, 0)),
            ]
            + [
                pl.BlockSpec(memory_space=pl.ANY),
                pl.BlockSpec((depth // nc, total, nc), lambda s, e: (0, 0, 0)),
            ][: len(given)],
            out_specs=[
                pl.BlockSpec((tile, nc, total), lambda s, e: (s + at, 0, 0)),
                pl.BlockSpec((depth // nc, total, nc), lambda s, e: (0, 0, 0)),
            ],
        ),
        out_shape=[
            pltpu.HBM((base.shape[0], nc, total), F32),
            pltpu.HBM((depth // nc, total, nc), F32),
        ],
        input_output_aliases={6: 0, 7: 1} if given else {},
        name="finish",
        **params(flops, size),
    )(eb, ec, ea, integrals, base, blocks, *given)


def energies(eps_occ, eps_virt, triple, energy_order):
    positions = jnp.arange(eps_virt.shape[0], dtype=jnp.int32)
    one_hot = energy_order[:, None] == positions[None, :]
    virt = jnp.sum(jnp.where(one_hot, eps_virt[None, :], F32(0.0)), axis=1)
    occ_positions = jnp.arange(eps_occ.shape[0], dtype=jnp.int32)
    occ_hot = triple[:, None] == occ_positions[None, :]
    occ = jnp.sum(jnp.where(occ_hot, eps_occ[None, :], F32(0.0)))
    return virt, occ


def tie(value, *after):
    return lax.optimization_barrier((value, after))[0]


def in_blocks(n, m, integrals, doubles, eps_occ, eps_virt, triple, energy_order):
    nb, nc, total = integrals.shape[1:]
    i = lax.axis_index("vb")
    j = lax.axis_index("vc")
    depth = total

    def over_b(x, k):
        return lax.ppermute(x, "vb", [(p, p ^ k) for p in range(n)]) if k else x

    def over_c(x, k):
        return lax.ppermute(x, "vc", [(p, p ^ k) for p in range(m)]) if k else x

    def all_over_b(x):
        return lax.all_to_all(x, "vb", split_axis=0, concat_axis=0, tiled=True)

    def in_order(pieces, place, axis):
        x = jnp.stack(pieces)
        ordered = [
            lax.dynamic_index_in_dim(x, place ^ p, 0, False) for p in range(len(pieces))
        ]
        return jnp.concatenate(ordered, axis=axis)

    few = max(nb // 16, 4)
    lots = [nb // 4, nb - nb // 4 - few, few]
    starts = [0, lots[0], lots[0] + lots[1]]

    share = depth // m
    own = doubles[1][: lots[0]]
    part = lax.dynamic_slice_in_dim(doubles, j * share, share, axis=2)
    far_rows = jnp.stack([over_b(own, k) for k in range(0, n, 2)])
    far_part = jnp.stack([over_b(part, k) for k in range(0, n, 2)])

    def from_last_bit(x):
        x = jnp.stack([x, over_b(x, 1)], axis=1)
        x = x.reshape((n,) + x.shape[2:])
        return jnp.stack([lax.dynamic_index_in_dim(x, i ^ p, 0, False) for p in range(n)])

    rows = from_last_bit(far_rows).reshape(n * lots[0], depth)
    half = nb // 2
    begun = second(integrals, (rows,), n, 0, half)
    far_part, begun = lax.optimization_barrier((far_part, tuple(begun)))
    part = from_last_bit(far_part)
    (lot,) = second(integrals, (rows,), n, half, nb - half, begun)
    part, lot = lax.optimization_barrier((part, lot))
    arrived = [all_over_b(lot)]

    part = part.reshape(n, 3, nb, share).transpose(1, 0, 2, 3).reshape(3, total, share)
    step, bits = m // 2, 0
    while step:
        part = jnp.stack([part, over_c(part, step)], axis=bits)
        step, bits = step // 2, bits + 1
    part = part.reshape((m,) + part.shape[bits:])
    full = in_order([part[q] for q in range(m)], j, 2)

    d2 = jnp.concatenate([lax.dynamic_slice_in_dim(full[2], (j ^ q) * nc, nc) for q in range(m)])
    thirds = third(integrals, d2, m)

    by_peer = full[1].reshape(n, nb, depth)
    rows = [
        by_peer[:, at : at + lot].reshape(n * lot, depth)
        for at, lot in zip(starts[1:], lots[1:])
    ]
    made = second(integrals, tie(tuple(rows), *thirds), n, 0, nb)
    thirds = [over_c(x, q) for q, x in enumerate(thirds)]
    made = tie(tuple(made), arrived[0])
    arrived.append(all_over_b(made[0]))

    virt, occ = energies(eps_occ, eps_virt, triple, energy_order)
    eb = occ - lax.dynamic_slice_in_dim(virt, i * nb, nb)
    ec = lax.dynamic_slice_in_dim(virt, j * nc, nc)[None, :]
    ea = jnp.broadcast_to(virt[:, None], (total, nc))
    offsets = jnp.stack([(j ^ q) * nc for q in range(m)]).astype(jnp.int32)
    base = first(integrals, full[0], offsets, thirds)

    given = finish(integrals, base, arrived[0], eb, ec, ea, starts[0], ())
    arrived.append(all_over_b(tie(made[1], arrived[1], given[1])))
    for blocks, at in zip(arrived[1:], starts[1:]):
        given = finish(integrals, base, blocks, eb, ec, ea, at, given)
    amplitudes, grad = given

    bit = j % 2
    pairs = grad.reshape(-1, 2, total, nc)
    keep = lax.dynamic_index_in_dim(pairs, bit, 1, False)
    give = lax.dynamic_index_in_dim(pairs, 1 - bit, 1, False)
    grad = keep + over_c(give, 1)
    grad = grad.reshape(m // 2, n, nb, nc).transpose(1, 0, 2, 3).reshape(n * m // 2, nb, nc)
    alike = [[p * m + q for p in range(n) for q in range(c, m, 2)] for c in range(2)]
    grad = lax.all_to_all(
        grad, ("vb", "vc"), split_axis=0, concat_axis=0, axis_index_groups=alike, tiled=True
    )
    return amplitudes, jnp.sum(grad, axis=0)


def plain(integrals, doubles, eps_occ, eps_virt, triple, energy_order):
    highest = lax.Precision.HIGHEST
    all_doubles = lax.all_gather(doubles, "vb", axis=1, tiled=True)
    k_block = integrals[0]
    i_block = integrals[1]
    nb, nc = k_block.shape[:2]
    first_term = jnp.einsum("pqd,ad->pqa", k_block, all_doubles[0], precision=highest)
    second_local = jnp.einsum("pqd,bd->bqp", k_block, all_doubles[1], precision=highest)
    second_term = lax.all_to_all(second_local, "vb", split_axis=0, concat_axis=2, tiled=True)
    third_local = jnp.einsum("pqd,cd->pcq", i_block, all_doubles[2], precision=highest)
    third_term = lax.all_to_all(third_local, "vc", split_axis=1, concat_axis=2, tiled=True)
    virt, occ = energies(eps_occ, eps_virt, triple, energy_order)
    eb = lax.dynamic_slice_in_dim(virt, lax.axis_index("vb") * nb, nb)
    ec = lax.dynamic_slice_in_dim(virt, lax.axis_index("vc") * nc, nc)
    low = occ - eb[:, None, None] - ec[None, :, None] - virt[None, None, :]
    amplitudes = (first_term + second_term + third_term) / low
    partial = jnp.einsum("bca,bcd->ad", amplitudes, k_block, precision=highest)
    rows = lax.psum_scatter(partial, "vb", scatter_dimension=0, tiled=True)
    grad = lax.psum_scatter(rows, "vc", scatter_dimension=1, tiled=True)
    return amplitudes, grad


def on_device(n, m, *args):
    nb, nc, total = args[0].shape[1:]
    power = n & (n - 1) == 0 and m & (m - 1) == 0
    fits = nc % LANES == 0 and nb % 32 == 0
    if power and fits:
        return in_blocks(n, m, *args)
    return plain(*args)


def solution(mesh):
    n, m = mesh.shape["vb"], mesh.shape["vc"]
    in_specs = (P(None, "vb", "vc", None), P(None, "vb", None), P(), P(), P(), P())
    out_specs = (P("vb", "vc", None), P("vb", "vc"))
    return jax.shard_map(
        functools.partial(on_device, n, m),
        mesh=mesh,
        in_specs=in_specs,
        out_specs=out_specs,
        check_vma=False,
    )
```
